256 devices in a mesh: span: 8 (over z_lo, y), chord: 32 (over x, z_hi, core).
Axes of the slice: x: 4, y: 4, z: 8 (z_hi: 4, z_lo: 2; z = z_hi * 2 + z_lo), core: 2. Of those that a mesh axis runs over, the one named last changes fastest.
Arguments:
- start_field: float32 [24, 64, 512, 256], P(None, 'span', 'chord'), may hold values from -6 to 6
- volume_source: float32 [24, 64, 512, 256], P(None, 'span', 'chord'), may hold values from -6 to 6
- stiff_class: int32 [64, 512, 256], P('span', 'chord'), may hold values from 0 to 7
- class_table: float32 [2, 8], replicated, may hold values from 0.3 to 3
- panel_sens: float32 [24, 8, 32768], P(None, 'span', 'chord'), may hold values from -18 to 18
- panel_owner: int32 [8, 32768, 1], P('span', 'chord'), may hold values from 0 to 31; in each aligned block of 1024 rows (0 to 1023, 1024 to 2047, ..., all dimensions but the last counted through in order) at most 128 rows name the same one
- panel_node: int32 [8, 32768], P('span', 'chord'), may hold values from 0 to 127
Outputs:
- final_field: float32 [24, 64, 512, 256], P(None, 'span', 'chord')
The draws below stay inside these ranges and needn't reach their ends.
Inputs may be any that keep to these rules, and one draw needn't show every extreme that they name: `panel_owner`: among the 1024 panels of one device no chord index is named by more than 128 panels, and some chord index is named by exactly 128. `panel_node`: span cell times 16 plus chord cell of a node in the wall layer of the receiving block.
All inputs are finite; a program needn't handle non-finite values.
Results may differ from the reference program's by a relative error of at most 0.00021.
Values sent between devices are 32-bit elements; how exact they have to be, the bound alone decides.
A program may use at most 128 MiB of HBM per device.

```python
import math
import jax
import jax.numpy as jnp
import numpy as np

FIELDS = 24
SWEEPS = 3
NCLASS = 8
CS = 8
CC = 16
K = 256
PANELS = 1024
CAP = 128
NS = 64
NC = 512
N_SPAN = 8
N_CHORD = 32


def with_ends(array, rng, low, largest):
    index_at = [jax.random.randint(jax.random.fold_in(rng, axis), (), 0, length) for axis, length in enumerate(array.shape)]
    main_axis = array.shape.index(max(array.shape))
    neighbour = index_at[:main_axis] + [(index_at[main_axis] + 1) % array.shape[main_axis]] + index_at[main_axis + 1:]
    return array.at[tuple(index_at)].set(low).at[tuple(neighbour)].set(largest)


def block_levels(rng, extent, shards, smallest, top_value):
    loudness, own = 1.0, jax.random.fold_in(rng, 6)
    for axis_at, blocks in shards:
        draws = jnp.exp(jax.random.uniform(jax.random.fold_in(own, axis_at), (blocks,), jnp.float32, smallest / len(shards), top_value / len(shards)))
        loudness = loudness * jnp.repeat(draws, extent[axis_at] // blocks).reshape([-1 if axis == axis_at else 1 for axis in range(len(extent))])
    return loudness


def deal_out(own_key, own, number, rows, amount, top, bound, lean):
    ranking = jax.random.permutation(own_key, amount)
    heavy_load, usual = shares(amount, rows * top, bound, lean, True), shares(amount, rows * top, bound, lean, False)
    places = jnp.arange(amount)

    def named(sizes, rotation):
        used = int((sizes > 0).sum())
        fixed = max(1, used // 4)
        moved = fixed + (places - fixed + rotation * (used - fixed)) % max(1, amount - fixed)
        return jnp.zeros((amount,), jnp.int32).at[ranking[jnp.where(places < fixed, places, moved)]].set(jnp.asarray(sizes, jnp.int32))

    sizes = jnp.where(number % 4 == 0, named(heavy_load, number // 4), named(usual, number - number // 4 - 1))
    mixed = jax.random.permutation(jax.random.fold_in(own, 3), amount)
    source_of, taker = mixed[0:amount // 2 * 2:2], mixed[1:amount // 2 * 2:2]
    margin = jnp.minimum(sizes[source_of] - 1, bound - sizes[taker]) // 2
    margin = jnp.where((source_of == ranking[0]) | (taker == ranking[0]) | (sizes[taker] == 0), 0, jnp.maximum(margin, 0))
    moved = jax.random.randint(jax.random.fold_in(own, 4), (amount // 2,), 0, 1 << 20) % (margin + 1)
    sizes = sizes.at[source_of].add(-moved).at[taker].add(moved)
    members = jnp.searchsorted(jnp.cumsum(sizes), jnp.arange(rows * top), side="right").astype(jnp.int32)
    grid = members.reshape(top, rows).T
    grid = grid[jax.random.permutation(jax.random.fold_in(own, 1), rows)]
    rotation = jax.random.randint(jax.random.fold_in(own, 2), (rows, 1), 0, top)
    return jnp.take_along_axis(grid, (jnp.arange(top)[None, :] + rotation) % top, axis=1)


def shares(number_of, total, reach, slope, full):
    weights = [(1 << 20) // math.isqrt(rank ** slope) + 1 for rank in range(1, number_of + 1)]
    largest = reach if full else min(reach, max(-(-total // number_of), total * weights[0] // sum(weights)))
    least = 1 if total - largest >= number_of - 1 else 0
    counts, surplus = [largest] + [least] * (number_of - 1), total - largest - least * (number_of - 1)
    while surplus > 0:
        free = [i for i in range(1, number_of) if counts[i] < largest] or [i for i in range(1, number_of) if counts[i] < reach]
        pool, budget = sum([weights[i] for i in free]), surplus
        for i in free:
            addition = min(reach - counts[i], max(1, budget * weights[i] // pool), surplus)
            counts[i] = counts[i] + addition
            surplus = surplus - addition
    return np.array(counts)


def centred(key, shape, width, bound, split=(), kind=jnp.bfloat16):
    entries = width * jax.random.normal(key, shape, jnp.float32)
    if split:
        entries = entries * block_levels(key, shape, split, -0.22, 0.18)
    return jnp.clip(entries, -bound, bound).astype(kind)


def setup_inputs(seed: int = 0) -> dict:
    arg_keys = jax.random.split(jax.random.key(seed), 8)
    start_field = centred(arg_keys[0], (FIELDS, NS, NC, K), 1.0, 6.0, ((1, 8), (2, 32)), jnp.float32)
    volume_source = centred(arg_keys[1], (FIELDS, NS, NC, K), 1.0, 6.0, ((1, 8), (2, 32)), jnp.float32)
    stiff_class = with_ends(jax.random.randint(arg_keys[2], (NS, NC, K), 0, NCLASS), jax.random.fold_in(arg_keys[2], 1), 0, NCLASS - 1).astype(jnp.int32)
    class_table = jnp.clip(jnp.exp(jax.random.uniform(arg_keys[3], (2, NCLASS), jnp.float32, math.log(0.3), math.log(3.0))), 0.3, 3.0)
    panel_sens = centred(arg_keys[4], (FIELDS, N_SPAN, N_CHORD * PANELS), 3.0, 18.0, ((1, 8), (2, 32)), jnp.float32)
    panel_owner_keys = jax.random.split(jax.random.fold_in(arg_keys[5], 1), N_SPAN * (N_CHORD * PANELS) // PANELS)
    panel_owner_turns = jax.random.permutation(jax.random.fold_in(arg_keys[5], 3), N_SPAN * (N_CHORD * PANELS) // PANELS)
    panel_owner = jax.vmap(lambda own, number: deal_out(jax.random.fold_in(arg_keys[5], 2), own, number, PANELS, N_CHORD, 1, CAP, 2))(panel_owner_keys, panel_owner_turns).reshape((N_SPAN, N_CHORD * PANELS, 1))
    panel_node = with_ends(jax.random.randint(arg_keys[6], (N_SPAN, N_CHORD * PANELS), 0, CS * CC), jax.random.fold_in(arg_keys[6], 1), 0, (CS * CC) - 1).astype(jnp.int32)
    return dict(start_field=start_field, volume_source=volume_source, stiff_class=stiff_class, class_table=class_table, panel_sens=panel_sens, panel_owner=panel_owner, panel_node=panel_node)


cheb_center = 1.0
cheb_half = 0.9


def sweep_parts(field_pad, coef_pad):
    mode_count = field_pad.shape[0] // 3
    interior = (slice(1, -1), slice(1, -1), slice(1, -1))
    shear_here = coef_pad[0][interior]
    bulk_here = coef_pad[1][interior]
    grid_shape = shear_here.shape
    center = field_pad[(slice(None),) + interior].reshape((mode_count, 3) + grid_shape)
    diagonal = jnp.zeros((3,) + grid_shape, jnp.float32)
    coupled = jnp.zeros_like(center)
    for direction in range(3):
        selector = (jnp.arange(3) == direction).astype(jnp.float32)[:, None, None, None]
        for first_at in (0, 2):
            beside = list(interior)
            beside[direction] = slice(first_at, first_at + grid_shape[direction])
            beside = tuple(beside)
            shear_part = 0.5 * (shear_here + coef_pad[0][beside])
            normal_part = 0.5 * (bulk_here + coef_pad[1][beside])
            weight = shear_part[None] + selector * normal_part[None]
            diagonal = diagonal + weight
            coupled = coupled + weight[None] * field_pad[(slice(None),) + beside].reshape(center.shape)
    applied = (diagonal[None] * center - coupled).reshape((mode_count * 3,) + grid_shape)
    return applied, diagonal


def jacobi_scale(residue, diagonal):
    mode_count = residue.shape[0] // 3
    return (residue.reshape((mode_count, 3) + diagonal.shape[1:]) / diagonal[None]).reshape(residue.shape)


def reference(start_field, volume_source, stiff_class, class_table, panel_sens, panel_owner, panel_node):
    shear = class_table[0][stiff_class]
    bulk = class_table[1][stiff_class]
    coef_pad = jnp.pad(jnp.stack([shear, bulk]), ((0, 0), (1, 1), (1, 1), (1, 1)))
    span_rows = jnp.broadcast_to(jnp.arange(N_SPAN, dtype=jnp.int32)[:, None], panel_node.shape)
    row_index = (span_rows * CS + panel_node // CC).reshape(-1)
    col_index = (panel_owner[:, :, 0] * CC + panel_node % CC).reshape(-1)
    wall_load = jnp.zeros((FIELDS, NS, NC), jnp.float32).at[:, row_index, col_index].add(panel_sens.reshape(FIELDS, -1))
    source = volume_source.at[:, :, :, 0].add(wall_load)
    current = start_field
    step_dir = jnp.zeros_like(start_field)
    rho = cheb_half / cheb_center
    for sweep in range(SWEEPS):
        applied, diagonal = sweep_parts(jnp.pad(current, ((0, 0), (1, 1), (1, 1), (1, 1))), coef_pad)
        scaled = jacobi_scale(source - applied, diagonal)
        if sweep == 0:
            step_dir = scaled / cheb_center
        else:
            rho_next = 1.0 / (2.0 * cheb_center / cheb_half - rho)
            step_dir = rho_next * rho * step_dir + (2.0 * rho_next / cheb_half) * scaled
            rho = rho_next
        current = current + step_dir
    return current
```

```python
import functools

import jax
import jax.numpy as jnp
from jax import lax
from jax.experimental import pallas as pl
from jax.experimental.pallas import tpu as pltpu
from jax.sharding import PartitionSpec as P

SWEEPS = 3
GROUPS = 4
CENTER = 1.0
HALF = 0.9
MESH = pl.DeviceIdType.MESH


def chebyshev():
    rho = HALF / CENTER
    out = [(1.0 / CENTER, 0.0)]
    for _ in range(SWEEPS - 1):
        rho_next = 1.0 / (2.0 * CENTER / HALF - rho)
        out.append((2.0 * rho_next / HALF, -rho_next * rho))
        rho = rho_next
    return out


def kernel(
    n_span, n_x, n_z,
    start, source, classes, table, sens, owner, node,
    out,
    u, src, cls, sens_v, owner_v, node_v, edge_out, edge_in, cls_edge_out, cls_edge_in,
    shear, bulk, shear_edge, bulk_edge, weights, split_sens, pick_node, part, part_core, part_x, part_z, wall,
    load_sem, halo_send, halo_recv, cls_send, cls_recv, core_sem, x_send, x_recv, z_send, z_recv,
):
    fields, span_cells, chord_cells, depth = start.shape
    panels = owner.shape[1]
    size = fields // GROUPS
    n_chord = 2 * n_x * n_z
    span, chord = lax.axis_index("span"), lax.axis_index("chord")
    my_x, my_z, my_core = chord // (2 * n_z), (chord // 2) % n_z, chord % 2

    def at(xi, zi, core):
        return (span, xi * (2 * n_z) + zi * 2 + core)

    exists = [span > 0, span < n_span - 1, chord > 0, chord < n_chord - 1]
    opposite = [1, 0, 3, 2]
    neighbour = [
        (jnp.maximum(span - 1, 0), chord),
        (jnp.minimum(span + 1, n_span - 1), chord),
        (span, jnp.maximum(chord - 1, 0)),
        (span, jnp.minimum(chord + 1, n_chord - 1)),
    ]
    x_peers = [lax.rem(my_x + d, n_x) for d in range(1, n_x)]
    z_peers = [lax.rem(my_z + d, n_z) for d in range(1, n_z)]

    def group(g):
        return pl.ds(pl.multiple_of(g * size, size), size)

    small = [
        pltpu.make_async_copy(classes, cls.at[pl.ds(1, span_cells)], load_sem.at[0]),
        pltpu.make_async_copy(owner, owner_v, load_sem.at[1]),
        pltpu.make_async_copy(node, node_v, load_sem.at[2]),
        pltpu.make_async_copy(sens, sens_v, load_sem.at[3]),
    ]
    field_loads = [
        pltpu.make_async_copy(
            start.at[pl.ds(g * size, size)],
            u.at[0, pl.ds(g * size, size), pl.ds(1, span_cells)],
            load_sem.at[4 + g],
        )
        for g in range(GROUPS)
    ]
    source_load = pltpu.make_async_copy(source, src, load_sem.at[4 + GROUPS])
    for copy in small + field_loads + [source_load]:
        copy.start()

    @pl.when(jnp.logical_not(exists[0]))
    def _():
        cls[0] = jnp.full(cls.shape[1:], -1, jnp.int32)
        for s in range(SWEEPS):
            for f in range(fields):
                u[s, f, 0] = jnp.zeros((chord_cells, depth), jnp.float32)

    @pl.when(jnp.logical_not(exists[1]))
    def _():
        cls[span_cells + 1] = jnp.full(cls.shape[1:], -1, jnp.int32)
        for s in range(SWEEPS):
            for f in range(fields):
                u[s, f, span_cells + 1] = jnp.zeros((chord_cells, depth), jnp.float32)

    for side in range(2):

        @pl.when(jnp.logical_not(exists[2 + side]))
        def _():
            cls_edge_in[side] = jnp.full(cls_edge_in.shape[1:], -1, jnp.int32)
            for s in range(SWEEPS):
                edge_in[s, side] = jnp.zeros(edge_in.shape[2:], jnp.float32)

    barrier = pltpu.get_barrier_semaphore()
    for d in range(4):

        @pl.when(exists[d])
        def _():
            pl.semaphore_signal(barrier, inc=1, device_id=neighbour[d], device_id_type=MESH)

    peers = [at(my_x, my_z, 1 - my_core)]
    peers += [at(xi, my_z, my_core) for xi in x_peers] + [at(my_x, zi, my_core) for zi in z_peers]
    for peer in peers:
        pl.semaphore_signal(barrier, inc=1, device_id=peer, device_id_type=MESH)
    count = sum(jnp.where(exists[d], 1, 0) for d in range(4))
    pl.semaphore_wait(barrier, count + len(peers))

    def class_copy(d):
        if d < 2:
            row = 0 if d == 0 else span_cells - 1
            from_ref = classes.at[pl.ds(row, 1)]
            to_ref = cls.at[pl.ds(span_cells + 1 if d == 0 else 0, 1)]
        else:
            from_ref, to_ref = cls_edge_out.at[d - 2], cls_edge_in.at[opposite[d] - 2]
        return pltpu.make_async_remote_copy(
            src_ref=from_ref, dst_ref=to_ref, send_sem=cls_send.at[d], recv_sem=cls_recv.at[d],
            device_id=neighbour[d], device_id_type=MESH,
        )

    def halo_copy(sweep, g, d):
        if d < 2:
            row = 0 if d == 0 else span_cells - 1
            if sweep == 0:
                from_ref = start.at[group(g), row]
            else:
                from_ref = u.at[sweep, group(g), row + 1]
            to_ref = u.at[sweep, group(g), span_cells + 1 if d == 0 else 0]
        else:
            from_ref = edge_out.at[sweep, d - 2, group(g)]
            to_ref = edge_in.at[sweep, opposite[d] - 2, group(g)]
        return pltpu.make_async_remote_copy(
            src_ref=from_ref, dst_ref=to_ref, send_sem=halo_send.at[sweep, g, d], recv_sem=halo_recv.at[sweep, g, d],
            device_id=neighbour[d], device_id_type=MESH,
        )

    def send(make, directions):
        for d in directions:

            @pl.when(exists[d])
            def _():
                make(d).start()

    def receive(make, directions):
        for d in directions:

            @pl.when(exists[opposite[d]])
            def _():
                make(d).wait_recv()

    send(class_copy, (0, 1))
    for g in range(GROUPS):
        send(functools.partial(halo_copy, 0, g), (0, 1))

    small[0].wait()
    for side, row in ((0, 0), (1, chord_cells - 1)):
        for s in range(span_cells):
            cls_edge_out[side, pl.ds(s, 1)] = cls[s + 1, pl.ds(row, 1)]
    send(class_copy, (2, 3))

    for g in range(GROUPS):
        field_loads[g].wait()

        @pl.loop(g * size, (g + 1) * size)
        def _(f):
            for side, row in ((0, 0), (1, chord_cells - 1)):
                for s in range(span_cells):
                    edge_out[0, side, f, pl.ds(s, 1)] = u[0, f, s + 1, pl.ds(row, 1)]

        send(functools.partial(halo_copy, 0, g), (2, 3))

    for copy in small[1:]:
        copy.wait()
    wall_nodes = pick_node.shape[0]
    values = sens_v[:, 0, :]
    high = values.astype(jnp.bfloat16).astype(jnp.float32)
    split_sens[...] = jnp.concatenate([high, values - high], axis=0).astype(jnp.bfloat16)
    nodes_at = lax.broadcasted_iota(jnp.int32, (wall_nodes, panels), 0)
    pick_node[...] = (nodes_at == node_v[...]).astype(jnp.float32).astype(jnp.bfloat16)

    def core_copy():
        return pltpu.make_async_remote_copy(
            src_ref=part.at[0], dst_ref=part_core, send_sem=core_sem.at[0], recv_sem=core_sem.at[1],
            device_id=at(my_x, my_z, 1 - my_core), device_id_type=MESH,
        )

    for half in range(2):
        core = 1 - my_core if half == 0 else my_core

        @pl.loop(0, n_x)
        def _(xi):
            rows = []
            for zi in range(n_z):
                mine = (owner_v[...] == xi * (2 * n_z) + zi * 2 + core).astype(jnp.float32).astype(jnp.bfloat16)
                rows.append(split_sens[...] * mine)
            sums = lax.dot_general(
                jnp.concatenate(rows, axis=0), pick_node[...], (((1,), (1,)), ((), ())),
                preferred_element_type=jnp.float32,
            )
            for zi in range(n_z):
                low = 2 * fields * zi
                part[half, xi, zi] = sums[low : low + fields] + sums[low + fields : low + 2 * fields]

        if half == 0:
            core_copy().start()

    receive(class_copy, range(4))

    def lookup(index):
        shear_here = jnp.zeros(index.shape, jnp.float32)
        bulk_here = jnp.zeros(index.shape, jnp.float32)
        for level in range(table.shape[1]):
            mask = index == level
            shear_here = jnp.where(mask, table[0, level], shear_here)
            bulk_here = jnp.where(mask, table[1, level], bulk_here)
        return shear_here, bulk_here

    for side in range(2):
        shear_edge[side], bulk_edge[side] = lookup(cls_edge_in[side])

    @pl.loop(0, span_cells + 2)
    def _(s):
        shear[s], bulk[s] = lookup(cls[s])

    row_at = lax.broadcasted_iota(jnp.int32, (chord_cells, depth), 0)
    lane_at = lax.broadcasted_iota(jnp.int32, (chord_cells, depth), 1)

    def beside_chord(values, low, high):
        return (
            jnp.where(row_at == 0, low, pltpu.roll(values, 1, 0)),
            jnp.where(row_at == chord_cells - 1, high, pltpu.roll(values, chord_cells - 1, 0)),
        )

    def beside_depth(values):
        return pltpu.roll(values, 1, 1), pltpu.roll(values, depth - 1, 1)

    @pl.loop(0, span_cells)
    def _(s):
        faces = []
        for coef, edge in ((shear, shear_edge), (bulk, bulk_edge)):
            here = coef[s + 1]
            beside = [coef[s], coef[s + 2]]
            beside += beside_chord(here, edge[0, pl.ds(s, 1)], edge[1, pl.ds(s, 1)])
            low, high = beside_depth(here)
            beside += [jnp.where(lane_at == 0, 0.0, low), jnp.where(lane_at == depth - 1, 0.0, high)]
            faces.append([0.5 * (here + there) for there in beside])
        total = functools.reduce(jnp.add, faces[0])
        for c in range(3):
            weights[12 + c, s] = 1.0 / (total + (faces[1][2 * c] + faces[1][2 * c + 1]))
        for e in range(6):
            normal = faces[0][e] + faces[1][e]
            tangent = faces[0][e]
            if e == 4:
                tangent, normal = (jnp.where(lane_at == 0, 0.0, w) for w in (tangent, normal))
            if e == 5:
                tangent, normal = (jnp.where(lane_at == depth - 1, 0.0, w) for w in (tangent, normal))
            weights[e, s] = tangent
            weights[6 + e, s] = normal

    core_copy().wait_recv()
    part[1] = part[1] + part_core[...]

    def x_copy(d):
        return pltpu.make_async_remote_copy(
            src_ref=part.at[1, x_peers[d]], dst_ref=part_x.at[d], send_sem=x_send.at[d], recv_sem=x_recv.at[d],
            device_id=at(x_peers[d], my_z, my_core), device_id_type=MESH,
        )

    def z_copy(d):
        return pltpu.make_async_remote_copy(
            src_ref=part_z.at[0, z_peers[d]], dst_ref=part_z.at[1, d], send_sem=z_send.at[d], recv_sem=z_recv.at[d],
            device_id=at(my_x, z_peers[d], my_core), device_id_type=MESH,
        )

    for d in range(n_x - 1):
        x_copy(d).start()
    total = part[1, my_x]
    for d in range(n_x - 1):
        x_copy(d).wait_recv()
        total = total + part_x[d]
    part_z[0] = total
    for d in range(n_z - 1):
        z_copy(d).start()
    total = part_z[0, my_z]
    for d in range(n_z - 1):
        z_copy(d).wait_recv()
        total = total + part_z[1, d]
    wall[...] = jnp.transpose(total)
    source_load.wait()
    first_lanes = lax.broadcasted_iota(jnp.int32, (span_cells, chord_cells, 128), 2)
    for f in range(fields):
        column = wall[:, pl.ds(f, 1)].reshape(span_cells, chord_cells, 1)
        src[f, :, :, pl.ds(0, 128)] = src[f, :, :, pl.ds(0, 128)] + jnp.where(first_lanes == 0, column, 0.0)

    steps = chebyshev()
    for sweep in range(SWEEPS):
        by_diag, by_old = steps[sweep]
        last = sweep == SWEEPS - 1

        def slab(g, s, sweep=sweep, by_diag=by_diag, by_old=by_old, last=last):
            for c in range(3):
                w = [weights[6 + e if e // 2 == c else e, s] for e in range(6)]
                scale = by_diag * weights[12 + c, s]
                for m in range(size // 3):
                    f = g * size + (3 * m + c)
                    here = u[sweep, f, s + 1]
                    row = pl.ds(s, 1)
                    beside = [u[sweep, f, s], u[sweep, f, s + 2]]
                    beside += beside_chord(here, edge_in[sweep, 0, f, row], edge_in[sweep, 1, f, row])
                    beside += beside_depth(here)
                    total = src[f, s]
                    for e in range(6):
                        total = total + w[e] * beside[e]
                    new = scale * total
                    if by_old != 0.0:
                        new = new + by_old * u[sweep - 1, f, s + 1]
                    if last:
                        out[f, s] = new
                    else:
                        u[sweep + 1, f, s + 1] = new
                        edge_out[sweep + 1, 0, f, row] = new[0:1]
                        edge_out[sweep + 1, 1, f, row] = new[chord_cells - 1 : chord_cells]

        @pl.loop(0, GROUPS)
        def _(g):
            receive(functools.partial(halo_copy, sweep, g), range(4))
            if last:

                @pl.loop(0, span_cells)
                def _(s):
                    slab(g, s)

            else:

                @pl.loop(0, 2)
                def _(i):
                    slab(g, i * (span_cells - 1))

                send(functools.partial(halo_copy, sweep + 1, g), (0, 1))

                @pl.loop(1, span_cells - 1)
                def _(s):
                    slab(g, s)

                send(functools.partial(halo_copy, sweep + 1, g), (2, 3))

    for d in range(4):

        @pl.when(exists[d])
        def _():
            class_copy(d).wait_send()
            for sweep in range(SWEEPS):

                @pl.loop(0, GROUPS)
                def _(g):
                    halo_copy(sweep, g, d).wait_send()

    core_copy().wait_send()
    for d in range(n_x - 1):
        x_copy(d).wait_send()
    for d in range(n_z - 1):
        z_copy(d).wait_send()


def body(n_span, n_x, n_z, start, source, classes, table, sens, owner, node):
    fields, span_cells, chord_cells, depth = start.shape
    panels = owner.shape[1]
    wall_nodes = span_cells * chord_cells
    f32, i32, bf16 = jnp.float32, jnp.int32, jnp.bfloat16
    dma = pltpu.SemaphoreType.DMA
    scratch = [
        pltpu.VMEM((SWEEPS, fields, span_cells + 2, chord_cells, depth), f32),
        pltpu.VMEM(start.shape, f32),
        pltpu.VMEM((span_cells + 2, chord_cells, depth), i32),
        pltpu.VMEM((fields, 1, panels), f32),
        pltpu.VMEM((1, panels), i32),
        pltpu.VMEM((1, panels), i32),
        pltpu.VMEM((SWEEPS, 2, fields, span_cells, depth), f32),
        pltpu.VMEM((SWEEPS, 2, fields, span_cells, depth), f32),
        pltpu.VMEM((2, span_cells, depth), i32),
        pltpu.VMEM((2, span_cells, depth), i32),
        pltpu.VMEM((span_cells + 2, chord_cells, depth), f32),
        pltpu.VMEM((span_cells + 2, chord_cells, depth), f32),
        pltpu.VMEM((2, span_cells, depth), f32),
        pltpu.VMEM((2, span_cells, depth), f32),
        pltpu.VMEM((15, span_cells, chord_cells, depth), f32),
        pltpu.VMEM((2 * fields, panels), bf16),
        pltpu.VMEM((wall_nodes, panels), bf16),
        pltpu.VMEM((2, n_x, n_z, fields, wall_nodes), f32),
        pltpu.VMEM((n_x, n_z, fields, wall_nodes), f32),
        pltpu.VMEM((n_x - 1, n_z, fields, wall_nodes), f32),
        pltpu.VMEM((2, n_z, fields, wall_nodes), f32),
        pltpu.VMEM((wall_nodes, fields), f32),
        dma((5 + GROUPS,)),
        dma((SWEEPS, GROUPS, 4)),
        dma((SWEEPS, GROUPS, 4)),
        dma((4,)),
        dma((4,)),
        dma((2,)),
        dma((n_x - 1,)),
        dma((n_x - 1,)),
        dma((n_z - 1,)),
        dma((n_z - 1,)),
    ]
    anywhere = pl.BlockSpec(memory_space=pl.ANY)
    return pl.pallas_call(
        functools.partial(kernel, n_span, n_x, n_z),
        out_shape=pltpu.VMEM(start.shape, f32),
        in_specs=[anywhere] * 3 + [pl.BlockSpec(memory_space=pltpu.SMEM)] + [anywhere] * 3,
        out_specs=pl.BlockSpec(memory_space=pltpu.VMEM),
        scratch_shapes=scratch,
        compiler_params=pltpu.CompilerParams(
            collective_id=0, has_side_effects=True, vmem_limit_bytes=48 * 1024 * 1024
        ),
    )(start, source, classes, table, sens, owner.reshape(1, panels), node)


def solution(mesh):
    n_span, n_chord = mesh.shape["span"], mesh.shape["chord"]
    n_x = n_z = round((n_chord // 2) ** 0.5)
    return jax.shard_map(
        functools.partial(body, n_span, n_x, n_z),
        mesh=mesh,
        in_specs=(
            P(None, "span", "chord", None),
            P(None, "span", "chord", None),
            P("span", "chord", None),
            P(),
            P(None, "span", "chord"),
            P("span", "chord", None),
            P("span", "chord"),
        ),
        out_specs=P(None, "span", "chord", None),
        check_vma=False,
    )
```

```python
import functools

import jax
import jax.numpy as jnp
from jax import lax
from jax.experimental import pallas as pl
from jax.experimental.pallas import tpu as pltpu
from jax.sharding import PartitionSpec as P

SWEEPS = 3
GROUPS = 4
CENTER = 1.0
HALF = 0.9
MESH = pl.DeviceIdType.MESH


def chebyshev():
    rho = HALF / CENTER
    out = [(1.0 / CENTER, 0.0)]
    for _ in range(SWEEPS - 1):
        rho_next = 1.0 / (2.0 * CENTER / HALF - rho)
        out.append((2.0 * rho_next / HALF, -rho_next * rho))
        rho = rho_next
    return out


def kernel(
    n_span, n_x, n_z,
    start, source, classes, table_in, sens, owner, node,
    out,
    table, u, src, cls, sens_v, owner_v, node_v, edge_out, edge_in, cls_edge_out, cls_edge_in, relayed,
    shear, bulk, shear_edge, bulk_edge, weights, split_sens, pick_node, part, part_core, part_x, part_z, wall,
    load_sem, halo_send, halo_recv, far_send, far_recv, hop_send, hop_recv, cls_send, cls_recv, core_sem, x_send, x_recv, z_send, z_recv,
):
    fields, span_cells, chord_cells, depth = start.shape
    panels = owner.shape[1]
    size = fields // GROUPS
    n_chord = 2 * n_x * n_z
    span, chord = lax.axis_index("span"), lax.axis_index("chord")
    my_x, my_z, my_core = chord // (2 * n_z), (chord // 2) % n_z, chord % 2

    def at(xi, zi, core):
        return (span, xi * (2 * n_z) + zi * 2 + core)

    exists = [span > 0, span < n_span - 1, chord > 0, chord < n_chord - 1]
    opposite = [1, 0, 3, 2]
    neighbour = [
        (jnp.maximum(span - 1, 0), chord),
        (jnp.minimum(span + 1, n_span - 1), chord),
        (span, jnp.maximum(chord - 1, 0)),
        (span, jnp.minimum(chord + 1, n_chord - 1)),
    ]
    middle = n_span // 2
    far = [span == middle, span == middle - 1]
    target = [middle - 1, middle]
    middle_of = [middle, middle - 1]
    relay_at = [n_span - 1, 0]
    half = size // 2
    x_peers = [lax.rem(my_x + d, n_x) for d in range(1, n_x)]
    z_peers = [lax.rem(my_z + d, n_z) for d in range(1, n_z)]

    def group(g, first=0, count=size):
        return pl.ds(g * size + first, count)

    barrier = pltpu.get_barrier_semaphore()
    for d in range(4):

        @pl.when(exists[d])
        def _():
            pl.semaphore_signal(barrier, inc=1, device_id=neighbour[d], device_id_type=MESH)

    for d in range(2):
        for ends in ((middle_of[d], relay_at[d]), (relay_at[d], target[d])):
            for here, there in (ends, ends[::-1]):

                @pl.when(span == here)
                def _():
                    pl.semaphore_signal(barrier, inc=1, device_id=(there, chord), device_id_type=MESH)

    peers = [at(my_x, my_z, 1 - my_core)]
    peers += [at(xi, my_z, my_core) for xi in x_peers] + [at(my_x, zi, my_core) for zi in z_peers]
    for peer in peers:
        pl.semaphore_signal(barrier, inc=1, device_id=peer, device_id_type=MESH)
    count = sum(jnp.where(exists[d], 1, 0) for d in range(4))
    count = count + sum(jnp.where(far[d], 2, 0) + jnp.where(span == relay_at[d], 2, 0) for d in range(2))

    small = [
        pltpu.make_async_copy(classes, cls.at[pl.ds(1, span_cells)], load_sem.at[0]),
        pltpu.make_async_copy(table_in, table, load_sem.at[5 + GROUPS]),
        pltpu.make_async_copy(owner, owner_v, load_sem.at[1]),
        pltpu.make_async_copy(node, node_v, load_sem.at[2]),
        pltpu.make_async_copy(sens, sens_v, load_sem.at[3]),
    ]
    field_loads = [
        pltpu.make_async_copy(
            start.at[pl.ds(g * size, size)],
            u.at[0, pl.ds(g * size, size), pl.ds(1, span_cells)],
            load_sem.at[4 + g],
        )
        for g in range(GROUPS)
    ]
    source_load = pltpu.make_async_copy(source, src, load_sem.at[4 + GROUPS])
    for copy in small + field_loads + [source_load]:
        copy.start()

    @pl.when(jnp.logical_not(exists[0]))
    def _():
        cls[0] = jnp.full(cls.shape[1:], -1, jnp.int32)
        for s in range(SWEEPS):
            for f in range(fields):
                u[s, f, 0] = jnp.zeros((chord_cells, depth), jnp.float32)

    @pl.when(jnp.logical_not(exists[1]))
    def _():
        cls[span_cells + 1] = jnp.full(cls.shape[1:], -1, jnp.int32)
        for s in range(SWEEPS):
            for f in range(fields):
                u[s, f, span_cells + 1] = jnp.zeros((chord_cells, depth), jnp.float32)

    for side in range(2):

        @pl.when(jnp.logical_not(exists[2 + side]))
        def _():
            cls_edge_in[side] = jnp.full(cls_edge_in.shape[1:], -1, jnp.int32)
            for s in range(SWEEPS):
                edge_in[s, side] = jnp.zeros(edge_in.shape[2:], jnp.float32)

    def class_copy(d):
        if d < 2:
            row = 0 if d == 0 else span_cells - 1
            from_ref = classes.at[pl.ds(row, 1)]
            to_ref = cls.at[pl.ds(span_cells + 1 if d == 0 else 0, 1)]
        else:
            from_ref, to_ref = cls_edge_out.at[d - 2], cls_edge_in.at[opposite[d] - 2]
        return pltpu.make_async_remote_copy(
            src_ref=from_ref, dst_ref=to_ref, send_sem=cls_send.at[d], recv_sem=cls_recv.at[d],
            device_id=neighbour[d], device_id_type=MESH,
        )

    everything, wall_side, inner_side = pl.ds(0, depth), pl.ds(0, depth // 2), pl.ds(depth // 2, depth // 2)
    inner, at_wall_side = (1, inner_side, SWEEPS), (1, wall_side, 1)
    parcels = [[(s, everything, s)] if s != 1 else [inner, at_wall_side] for s in range(SWEEPS)]

    def outer_row(parcel, d, some):
        sweep, lanes, _ = parcel
        row = 0 if d == 0 else span_cells - 1
        return start.at[some, row, :, lanes] if sweep == 0 else u.at[sweep, some, row + 1, :, lanes]

    def halo_row(parcel, d, some):
        sweep, lanes, _ = parcel
        return u.at[sweep, some, span_cells + 1 if d == 0 else 0, :, lanes]

    def halo_copy(parcel, g, d, count=size):
        sweep, lanes, slot = parcel
        if d < 2:
            some = group(g, 0, count)
            from_ref, to_ref = outer_row(parcel, d, some), halo_row(parcel, d, some)
        else:
            from_ref = edge_out.at[sweep, d - 2, group(g), :, lanes]
            to_ref = edge_in.at[sweep, opposite[d] - 2, group(g), :, lanes]
        return pltpu.make_async_remote_copy(
            src_ref=from_ref, dst_ref=to_ref, send_sem=halo_send.at[slot, g, d], recv_sem=halo_recv.at[slot, g, d],
            device_id=neighbour[d], device_id_type=MESH,
        )

    def far_copy(parcel, g, d):
        sweep, lanes, slot = parcel
        return pltpu.make_async_remote_copy(
            src_ref=outer_row(parcel, d, group(g, half, half)), dst_ref=relayed.at[sweep, g, :, :, lanes],
            send_sem=far_send.at[slot, g], recv_sem=far_recv.at[slot, g],
            device_id=(relay_at[d], chord), device_id_type=MESH,
        )

    def hop_copy(parcel, g, d):
        sweep, lanes, slot = parcel
        return pltpu.make_async_remote_copy(
            src_ref=relayed.at[sweep, g, :, :, lanes], dst_ref=halo_row(parcel, d, group(g, half, half)),
            send_sem=hop_send.at[slot, g], recv_sem=hop_recv.at[slot, g],
            device_id=(target[d], chord), device_id_type=MESH,
        )

    def when(condition, *actions):
        @pl.when(condition)
        def _():
            for action in actions:
                action()

    def send_class(directions):
        for d in directions:
            when(exists[d], class_copy(d).start)

    def send_halo(parcel, g, directions):
        for d in directions:
            if d < 2:
                when(far[d], lambda: far_copy(parcel, g, d).start(), lambda: halo_copy(parcel, g, d, half).start())
                when(exists[d] & jnp.logical_not(far[d]), lambda: halo_copy(parcel, g, d).start())
            else:
                when(exists[d], lambda: halo_copy(parcel, g, d).start())

    def receive_halo(sweep, g, directions):
        for d in directions:
            back = opposite[d]
            for parcel in parcels[sweep]:
                if d < 2:
                    when(
                        far[back],
                        lambda: halo_copy(parcel, g, d, half).wait_recv(),
                        lambda: hop_copy(parcel, g, d).wait_recv(),
                    )
                    when(exists[back] & jnp.logical_not(far[back]), lambda: halo_copy(parcel, g, d).wait_recv())
                else:
                    when(exists[back], lambda: halo_copy(parcel, g, d).wait_recv())

    def relay(parcel, g):
        for d in range(2):
            when(span == relay_at[d], lambda: far_copy(parcel, g, d).wait_recv(), lambda: hop_copy(parcel, g, d).start())

    for copy in small[1:]:
        copy.wait()
    wall_nodes = pick_node.shape[0]
    values = sens_v[:, 0, :]
    high = values.astype(jnp.bfloat16).astype(jnp.float32)
    split_sens[...] = jnp.concatenate([high, values - high], axis=0).astype(jnp.bfloat16)
    nodes_at = lax.broadcasted_iota(jnp.int32, (wall_nodes, panels), 0)
    pick_node[...] = (nodes_at == node_v[...]).astype(jnp.float32).astype(jnp.bfloat16)

    for turn in range(2):
        core = 1 - my_core if turn == 0 else my_core

        @pl.loop(0, n_x)
        def _(xi):
            rows = []
            for zi in range(n_z):
                mine = (owner_v[...] == xi * (2 * n_z) + zi * 2 + core).astype(jnp.float32).astype(jnp.bfloat16)
                rows.append(split_sens[...] * mine)
            sums = lax.dot_general(
                jnp.concatenate(rows, axis=0), pick_node[...], (((1,), (1,)), ((), ())),
                preferred_element_type=jnp.float32,
            )
            for zi in range(n_z):
                low = 2 * fields * zi
                part[turn, xi, zi] = sums[low : low + fields] + sums[low + fields : low + 2 * fields]

    def core_copy():
        return pltpu.make_async_remote_copy(
            src_ref=part.at[0], dst_ref=part_core, send_sem=core_sem.at[0], recv_sem=core_sem.at[1],
            device_id=at(my_x, my_z, 1 - my_core), device_id_type=MESH,
        )

    def x_copy(d):
        return pltpu.make_async_remote_copy(
            src_ref=part.at[1, x_peers[d]], dst_ref=part_x.at[d], send_sem=x_send.at[d], recv_sem=x_recv.at[d],
            device_id=at(x_peers[d], my_z, my_core), device_id_type=MESH,
        )

    def z_copy(d):
        return pltpu.make_async_remote_copy(
            src_ref=part_z.at[0, z_peers[d]], dst_ref=part_z.at[1, d], send_sem=z_send.at[d], recv_sem=z_recv.at[d],
            device_id=at(my_x, z_peers[d], my_core), device_id_type=MESH,
        )

    pl.semaphore_wait(barrier, count + len(peers))
    core_copy().start()
    send_class((0, 1))
    for g in range(GROUPS):
        send_halo(parcels[0][0], g, (0, 1))

    def pack_edges(sweep, g, lanes):
        @pl.loop(g * size, (g + 1) * size)
        def _(f):
            for side, row in ((0, 0), (1, chord_cells - 1)):
                for s in range(span_cells):
                    edge_out[sweep, side, f, pl.ds(s, 1), lanes] = u[sweep, f, s + 1, pl.ds(row, 1), lanes]

    small[0].wait()
    for side, row in ((0, 0), (1, chord_cells - 1)):
        for s in range(span_cells):
            cls_edge_out[side, pl.ds(s, 1)] = cls[s + 1, pl.ds(row, 1)]
    send_class((2, 3))

    for g in range(GROUPS):
        field_loads[g].wait()
        pack_edges(0, g, everything)
        send_halo(parcels[0][0], g, (2, 3))

    core_copy().wait_recv()
    part[1] = part[1] + part_core[...]

    for d in range(n_x - 1):
        x_copy(d).start()
    for g in range(GROUPS):
        relay(parcels[0][0], g)

    for d in range(4):
        when(exists[opposite[d]], class_copy(d).wait_recv)

    def lookup(index):
        shear_here = jnp.zeros(index.shape, jnp.float32)
        bulk_here = jnp.zeros(index.shape, jnp.float32)
        for level in range(table.shape[1]):
            mask = index == level
            shear_here = jnp.where(mask, table[0, level], shear_here)
            bulk_here = jnp.where(mask, table[1, level], bulk_here)
        return shear_here, bulk_here

    for side in range(2):
        shear_edge[side], bulk_edge[side] = lookup(cls_edge_in[side])

    @pl.loop(0, span_cells + 2)
    def _(s):
        shear[s], bulk[s] = lookup(cls[s])

    row_at = lax.broadcasted_iota(jnp.int32, (chord_cells, depth), 0)
    lane_at = lax.broadcasted_iota(jnp.int32, (chord_cells, depth), 1)

    def beside_chord(values, low, high):
        return (
            jnp.where(row_at == 0, low, pltpu.roll(values, 1, 0)),
            jnp.where(row_at == chord_cells - 1, high, pltpu.roll(values, chord_cells - 1, 0)),
        )

    def beside_depth(values):
        return pltpu.roll(values, 1, 1), pltpu.roll(values, depth - 1, 1)

    @pl.loop(0, span_cells)
    def _(s):
        faces = []
        for coef, edge in ((shear, shear_edge), (bulk, bulk_edge)):
            here = coef[s + 1]
            beside = [coef[s], coef[s + 2]]
            beside += beside_chord(here, edge[0, pl.ds(s, 1)], edge[1, pl.ds(s, 1)])
            low, high = beside_depth(here)
            beside += [jnp.where(lane_at == 0, 0.0, low), jnp.where(lane_at == depth - 1, 0.0, high)]
            faces.append([0.5 * (here + there) for there in beside])
        total = functools.reduce(jnp.add, faces[0])
        for c in range(3):
            weights[12 + c, s] = 1.0 / (total + (faces[1][2 * c] + faces[1][2 * c + 1]))
        for e in range(6):
            normal = faces[0][e] + faces[1][e]
            tangent = faces[0][e]
            if e == 4:
                tangent, normal = (jnp.where(lane_at == 0, 0.0, w) for w in (tangent, normal))
            if e == 5:
                tangent, normal = (jnp.where(lane_at == depth - 1, 0.0, w) for w in (tangent, normal))
            weights[e, s] = tangent
            weights[6 + e, s] = normal

    total = part[1, my_x]
    for d in range(n_x - 1):
        x_copy(d).wait_recv()
        total = total + part_x[d]
    part_z[0] = total
    for d in range(n_z - 1):
        z_copy(d).start()

    steps = chebyshev()

    def slab(sweep, g, s):
        by_diag, by_old = steps[sweep]
        for c in range(3):
            w = [weights[6 + e if e // 2 == c else e, s] for e in range(6)]
            scale = by_diag * weights[12 + c, s]
            for m in range(size // 3):
                f = g * size + (3 * m + c)
                here = u[sweep, f, s + 1]
                row = pl.ds(s, 1)
                beside = [u[sweep, f, s], u[sweep, f, s + 2]]
                beside += beside_chord(here, edge_in[sweep, 0, f, row], edge_in[sweep, 1, f, row])
                beside += beside_depth(here)
                total = src[f, s]
                for e in range(6):
                    total = total + w[e] * beside[e]
                new = scale * total
                if by_old != 0.0:
                    new = new + by_old * u[sweep - 1, f, s + 1]
                if sweep == SWEEPS - 1:
                    out[f, s] = new
                else:
                    u[sweep + 1, f, s + 1] = new
                    edge_out[sweep + 1, 0, f, row] = new[0:1]
                    edge_out[sweep + 1, 1, f, row] = new[chord_cells - 1 : chord_cells]

    source_load.wait()

    @pl.loop(0, GROUPS)
    def _(g):
        receive_halo(0, g, range(4))

        @pl.loop(0, 2)
        def _(i):
            slab(0, g, i * (span_cells - 1))

        send_halo(inner, g, (0, 1))

        @pl.loop(1, span_cells - 1)
        def _(s):
            slab(0, g, s)

        send_halo(inner, g, (2, 3))

        @pl.when(g > 0)
        def _():
            relay(inner, g - 1)

    relay(inner, GROUPS - 1)

    total = part_z[0, my_z]
    for d in range(n_z - 1):
        z_copy(d).wait_recv()
        total = total + part_z[1, d]
    wall[...] = jnp.transpose(total)
    at_wall = lax.broadcasted_iota(jnp.int32, (span_cells, chord_cells, 128), 2) == 0
    lanes = pl.ds(0, 128)
    rows = pl.ds(1, span_cells)
    for g in range(GROUPS):
        for c in range(3):
            scale = steps[0][0] * weights[12 + c, :, :, lanes]
            for m in range(size // 3):
                f = g * size + 3 * m + c
                column = wall[:, pl.ds(f, 1)].reshape(span_cells, chord_cells, 1)
                load = jnp.where(at_wall, column, 0.0)
                src[f, :, :, lanes] = src[f, :, :, lanes] + load
                u[1, f, rows, :, lanes] = u[1, f, rows, :, lanes] + scale * load
        send_halo(at_wall_side, g, (0, 1))
        pack_edges(1, g, wall_side)
        send_halo(at_wall_side, g, (2, 3))
        if g > 0:
            relay(at_wall_side, g - 1)
    relay(at_wall_side, GROUPS - 1)

    for sweep in range(1, SWEEPS - 1):
        parcel = parcels[sweep + 1][0]

        @pl.loop(0, GROUPS)
        def _(g):
            receive_halo(sweep, g, range(4))

            @pl.loop(0, 2)
            def _(i):
                slab(sweep, g, i * (span_cells - 1))

            send_halo(parcel, g, (0, 1))

            @pl.loop(1, span_cells - 1)
            def _(s):
                slab(sweep, g, s)

            send_halo(parcel, g, (2, 3))

            @pl.when(g > 0)
            def _():
                relay(parcel, g - 1)

        relay(parcel, GROUPS - 1)

    @pl.loop(0, GROUPS)
    def _(g):
        receive_halo(SWEEPS - 1, g, (2, 3))

        @pl.loop(1, span_cells - 1)
        def _(s):
            slab(SWEEPS - 1, g, s)

        receive_halo(SWEEPS - 1, g, (0, 1))

        @pl.loop(0, 2)
        def _(i):
            slab(SWEEPS - 1, g, i * (span_cells - 1))

    for d in range(4):
        when(exists[d], class_copy(d).wait_send)

    for parcel in sum(parcels, []):

        @pl.loop(0, GROUPS)
        def _(g):
            for d in range(4):
                if d < 2:
                    when(
                        far[d],
                        lambda: far_copy(parcel, g, d).wait_send(),
                        lambda: halo_copy(parcel, g, d, half).wait_send(),
                    )
                    when(span == relay_at[d], lambda: hop_copy(parcel, g, d).wait_send())
                    when(exists[d] & jnp.logical_not(far[d]), lambda: halo_copy(parcel, g, d).wait_send())
                else:
                    when(exists[d], lambda: halo_copy(parcel, g, d).wait_send())

    core_copy().wait_send()
    for d in range(n_x - 1):
        x_copy(d).wait_send()
    for d in range(n_z - 1):
        z_copy(d).wait_send()


def body(n_span, n_x, n_z, start, source, classes, table, sens, owner, node):
    fields, span_cells, chord_cells, depth = start.shape
    panels = owner.shape[1]
    wall_nodes = span_cells * chord_cells
    half = fields // GROUPS // 2
    f32, i32, bf16 = jnp.float32, jnp.int32, jnp.bfloat16
    dma = pltpu.SemaphoreType.DMA
    scratch = [
        pltpu.SMEM(table.shape, f32),
        pltpu.VMEM((SWEEPS, fields, span_cells + 2, chord_cells, depth), f32),
        pltpu.VMEM(start.shape, f32),
        pltpu.VMEM((span_cells + 2, chord_cells, depth), i32),
        pltpu.VMEM((fields, 1, panels), f32),
        pltpu.VMEM((1, panels), i32),
        pltpu.VMEM((1, panels), i32),
        pltpu.VMEM((SWEEPS, 2, fields, span_cells, depth), f32),
        pltpu.VMEM((SWEEPS, 2, fields, span_cells, depth), f32),
        pltpu.VMEM((2, span_cells, depth), i32),
        pltpu.VMEM((2, span_cells, depth), i32),
        pltpu.VMEM((SWEEPS, GROUPS, half, chord_cells, depth), f32),
        pltpu.VMEM((span_cells + 2, chord_cells, depth), f32),
        pltpu.VMEM((span_cells + 2, chord_cells, depth), f32),
        pltpu.VMEM((2, span_cells, depth), f32),
        pltpu.VMEM((2, span_cells, depth), f32),
        pltpu.VMEM((15, span_cells, chord_cells, depth), f32),
        pltpu.VMEM((2 * fields, panels), bf16),
        pltpu.VMEM((wall_nodes, panels), bf16),
        pltpu.VMEM((2, n_x, n_z, fields, wall_nodes), f32),
        pltpu.VMEM((n_x, n_z, fields, wall_nodes), f32),
        pltpu.VMEM((n_x - 1, n_z, fields, wall_nodes), f32),
        pltpu.VMEM((2, n_z, fields, wall_nodes), f32),
        pltpu.VMEM((wall_nodes, fields), f32),
        dma((6 + GROUPS,)),
        dma((SWEEPS + 1, GROUPS, 4)),
        dma((SWEEPS + 1, GROUPS, 4)),
        dma((SWEEPS + 1, GROUPS)),
        dma((SWEEPS + 1, GROUPS)),
        dma((SWEEPS + 1, GROUPS)),
        dma((SWEEPS + 1, GROUPS)),
        dma((4,)),
        dma((4,)),
        dma((2,)),
        dma((n_x - 1,)),
        dma((n_x - 1,)),
        dma((n_z - 1,)),
        dma((n_z - 1,)),
    ]
    operands = (start, source, classes, table, sens, owner.reshape(1, panels), node)
    anywhere = pl.BlockSpec(memory_space=pl.ANY)
    return pl.pallas_call(
        functools.partial(kernel, n_span, n_x, n_z),
        out_shape=pltpu.VMEM(start.shape, f32),
        in_specs=[anywhere] * 7,
        out_specs=pl.BlockSpec(memory_space=pltpu.VMEM),
        scratch_shapes=scratch,
        compiler_params=pltpu.CompilerParams(
            collective_id=0, has_side_effects=True, vmem_limit_bytes=48 * 1024 * 1024
        ),
    )(*[pltpu.with_memory_space_constraint(array, pltpu.HBM) for array in operands])


def solution(mesh):
    n_span, n_chord = mesh.shape["span"], mesh.shape["chord"]
    n_x = n_z = round((n_chord // 2) ** 0.5)
    return jax.shard_map(
        functools.partial(body, n_span, n_x, n_z),
        mesh=mesh,
        in_specs=(
            P(None, "span", "chord", None),
            P(None, "span", "chord", None),
            P("span", "chord", None),
            P(),
            P(None, "span", "chord"),
            P("span", "chord", None),
            P("span", "chord"),
        ),
        out_specs=P(None, "span", "chord", None),
        check_vma=False,
    )
```

```python
import functools

import jax
import jax.numpy as jnp
from jax import lax
from jax.experimental import pallas as pl
from jax.experimental.pallas import tpu as pltpu
from jax.sharding import PartitionSpec as P

SWEEPS = 3
GROUPS = 2
RELAYED = (6, 6, 6, 6)
CENTER = 1.0
HALF = 0.9
MESH = pl.DeviceIdType.MESH


def chebyshev():
    rho = HALF / CENTER
    out = [(1.0 / CENTER, 0.0)]
    for _ in range(SWEEPS - 1):
        rho_next = 1.0 / (2.0 * CENTER / HALF - rho)
        out.append((2.0 * rho_next / HALF, -rho_next * rho))
        rho = rho_next
    return out


def kernel(
    n_span, n_x, n_z,
    start, source, classes, table_in, sens, owner, node,
    out,
    table, u, src, cls, sens_v, owner_v, node_v, edge_out, edge_in, cls_edge_out, cls_edge_in, relayed,
    shear, bulk, shear_edge, bulk_edge, weights, split_sens, pick_node, part, part_core, part_x, part_z, wall,
    load_sem, halo_send, halo_recv, far_send, far_recv, hop_send, hop_recv, cls_send, cls_recv, core_sem, x_send, x_recv, z_send, z_recv,
):
    fields, span_cells, chord_cells, depth = start.shape
    panels = owner.shape[1]
    size = fields // GROUPS
    n_chord = 2 * n_x * n_z
    span, chord = lax.axis_index("span"), lax.axis_index("chord")
    my_x, my_z, my_core = chord // (2 * n_z), (chord // 2) % n_z, chord % 2

    def at(xi, zi, core):
        return (span, xi * (2 * n_z) + zi * 2 + core)

    exists = [span > 0, span < n_span - 1, chord > 0, chord < n_chord - 1]
    opposite = [1, 0, 3, 2]
    neighbour = [
        (jnp.maximum(span - 1, 0), chord),
        (jnp.minimum(span + 1, n_span - 1), chord),
        (span, jnp.maximum(chord - 1, 0)),
        (span, jnp.minimum(chord + 1, n_chord - 1)),
    ]
    middle = n_span // 2
    far = [span == middle, span == middle - 1]
    target = [middle - 1, middle]
    middle_of = [middle, middle - 1]
    relay_at = [n_span - 1, 0]
    x_peers = [lax.rem(my_x + d, n_x) for d in range(1, n_x)]
    z_peers = [lax.rem(my_z + d, n_z) for d in range(1, n_z)]

    def group(g, first=0, count=size):
        return pl.ds(g * size + first, count)

    barrier = pltpu.get_barrier_semaphore()
    for d in range(4):

        @pl.when(exists[d])
        def _():
            pl.semaphore_signal(barrier, inc=1, device_id=neighbour[d], device_id_type=MESH)

    for d in range(2):
        for ends in ((middle_of[d], relay_at[d]), (relay_at[d], target[d])):
            for here, there in (ends, ends[::-1]):

                @pl.when(span == here)
                def _():
                    pl.semaphore_signal(barrier, inc=1, device_id=(there, chord), device_id_type=MESH)

    peers = [at(my_x, my_z, 1 - my_core)]
    peers += [at(xi, my_z, my_core) for xi in x_peers] + [at(my_x, zi, my_core) for zi in z_peers]
    for peer in peers:
        pl.semaphore_signal(barrier, inc=1, device_id=peer, device_id_type=MESH)
    count = sum(jnp.where(exists[d], 1, 0) for d in range(4))
    count = count + sum(jnp.where(far[d], 2, 0) + jnp.where(span == relay_at[d], 2, 0) for d in range(2))

    small = [
        pltpu.make_async_copy(classes, cls.at[pl.ds(1, span_cells)], load_sem.at[0]),
        pltpu.make_async_copy(table_in, table, load_sem.at[5 + GROUPS]),
        pltpu.make_async_copy(owner, owner_v, load_sem.at[1]),
        pltpu.make_async_copy(node, node_v, load_sem.at[2]),
        pltpu.make_async_copy(sens, sens_v, load_sem.at[3]),
    ]
    field_loads = [
        pltpu.make_async_copy(
            start.at[pl.ds(g * size, size)],
            u.at[0, pl.ds(g * size, size), pl.ds(1, span_cells)],
            load_sem.at[4 + g],
        )
        for g in range(GROUPS)
    ]
    source_load = pltpu.make_async_copy(source, src, load_sem.at[4 + GROUPS])
    for copy in small + field_loads + [source_load]:
        copy.start()

    @pl.when(jnp.logical_not(exists[0]))
    def _():
        cls[0] = jnp.full(cls.shape[1:], -1, jnp.int32)
        for s in range(SWEEPS):
            for f in range(fields):
                u[s, f, 0] = jnp.zeros((chord_cells, depth), jnp.float32)

    @pl.when(jnp.logical_not(exists[1]))
    def _():
        cls[span_cells + 1] = jnp.full(cls.shape[1:], -1, jnp.int32)
        for s in range(SWEEPS):
            for f in range(fields):
                u[s, f, span_cells + 1] = jnp.zeros((chord_cells, depth), jnp.float32)

    for side in range(2):

        @pl.when(jnp.logical_not(exists[2 + side]))
        def _():
            cls_edge_in[side] = jnp.full(cls_edge_in.shape[1:], -1, jnp.int32)
            for s in range(SWEEPS):
                edge_in[s, side] = jnp.zeros(edge_in.shape[2:], jnp.float32)

    def class_copy(d):
        if d < 2:
            row = 0 if d == 0 else span_cells - 1
            from_ref = classes.at[pl.ds(row, 1)]
            to_ref = cls.at[pl.ds(span_cells + 1 if d == 0 else 0, 1)]
        else:
            from_ref, to_ref = cls_edge_out.at[d - 2], cls_edge_in.at[opposite[d] - 2]
        return pltpu.make_async_remote_copy(
            src_ref=from_ref, dst_ref=to_ref, send_sem=cls_send.at[d], recv_sem=cls_recv.at[d],
            device_id=neighbour[d], device_id_type=MESH,
        )

    everything, wall_side, inner_side = pl.ds(0, depth), pl.ds(0, depth // 2), pl.ds(depth // 2, depth // 2)
    inner, at_wall_side = (1, inner_side, SWEEPS), (1, wall_side, 1)
    parcels = [[(s, everything, s)] if s != 1 else [inner, at_wall_side] for s in range(SWEEPS)]

    def outer_row(parcel, d, some):
        sweep, lanes, _ = parcel
        row = 0 if d == 0 else span_cells - 1
        return start.at[some, row, :, lanes] if sweep == 0 else u.at[sweep, some, row + 1, :, lanes]

    def halo_row(parcel, d, some):
        sweep, lanes, _ = parcel
        return u.at[sweep, some, span_cells + 1 if d == 0 else 0, :, lanes]

    def halo_copy(parcel, g, d, relay_too=False):
        sweep, lanes, slot = parcel
        if d < 2:
            some = group(g, 0, size - RELAYED[slot] if relay_too else size)
            from_ref, to_ref = outer_row(parcel, d, some), halo_row(parcel, d, some)
        else:
            from_ref = edge_out.at[sweep, d - 2, group(g), :, lanes]
            to_ref = edge_in.at[sweep, opposite[d] - 2, group(g), :, lanes]
        return pltpu.make_async_remote_copy(
            src_ref=from_ref, dst_ref=to_ref, send_sem=halo_send.at[slot, g, d], recv_sem=halo_recv.at[slot, g, d],
            device_id=neighbour[d], device_id_type=MESH,
        )

    def relay_fields(slot, g):
        return group(g, size - RELAYED[slot], RELAYED[slot])

    def far_copy(parcel, g, d):
        sweep, lanes, slot = parcel
        return pltpu.make_async_remote_copy(
            src_ref=outer_row(parcel, d, relay_fields(slot, g)),
            dst_ref=relayed.at[sweep, g, pl.ds(0, RELAYED[slot]), :, lanes],
            send_sem=far_send.at[slot, g], recv_sem=far_recv.at[slot, g],
            device_id=(relay_at[d], chord), device_id_type=MESH,
        )

    def hop_copy(parcel, g, d):
        sweep, lanes, slot = parcel
        return pltpu.make_async_remote_copy(
            src_ref=relayed.at[sweep, g, pl.ds(0, RELAYED[slot]), :, lanes],
            dst_ref=halo_row(parcel, d, relay_fields(slot, g)),
            send_sem=hop_send.at[slot, g], recv_sem=hop_recv.at[slot, g],
            device_id=(target[d], chord), device_id_type=MESH,
        )

    def when(condition, *actions):
        @pl.when(condition)
        def _():
            for action in actions:
                action()

    def send_class(directions):
        for d in directions:
            when(exists[d], class_copy(d).start)

    def send_halo(parcel, g, directions):
        for d in directions:
            if d < 2:
                when(far[d], lambda: far_copy(parcel, g, d).start(), lambda: halo_copy(parcel, g, d, True).start())
                when(exists[d] & jnp.logical_not(far[d]), lambda: halo_copy(parcel, g, d).start())
            else:
                when(exists[d], lambda: halo_copy(parcel, g, d).start())

    def receive_halo(sweep, g, directions):
        for d in directions:
            back = opposite[d]
            for parcel in parcels[sweep]:
                if d < 2:
                    when(
                        far[back],
                        lambda: halo_copy(parcel, g, d, True).wait_recv(),
                        lambda: hop_copy(parcel, g, d).wait_recv(),
                    )
                    when(exists[back] & jnp.logical_not(far[back]), lambda: halo_copy(parcel, g, d).wait_recv())
                else:
                    when(exists[back], lambda: halo_copy(parcel, g, d).wait_recv())

    def relay(parcel, g):
        for d in range(2):
            when(span == relay_at[d], lambda: far_copy(parcel, g, d).wait_recv(), lambda: hop_copy(parcel, g, d).start())

    def core_copy():
        return pltpu.make_async_remote_copy(
            src_ref=part.at[0], dst_ref=part_core, send_sem=core_sem.at[0], recv_sem=core_sem.at[1],
            device_id=at(my_x, my_z, 1 - my_core), device_id_type=MESH,
        )

    def x_copy(d):
        return pltpu.make_async_remote_copy(
            src_ref=part.at[1, x_peers[d]], dst_ref=part_x.at[d], send_sem=x_send.at[d], recv_sem=x_recv.at[d],
            device_id=at(x_peers[d], my_z, my_core), device_id_type=MESH,
        )

    def z_copy(d):
        return pltpu.make_async_remote_copy(
            src_ref=part_z.at[0, z_peers[d]], dst_ref=part_z.at[1, d], send_sem=z_send.at[d], recv_sem=z_recv.at[d],
            device_id=at(my_x, z_peers[d], my_core), device_id_type=MESH,
        )

    def pack_edges(sweep, g, lanes):
        @pl.loop(g * size, (g + 1) * size)
        def _(f):
            for side, row in ((0, 0), (1, chord_cells - 1)):
                for s in range(span_cells):
                    edge_out[sweep, side, f, pl.ds(s, 1), lanes] = u[sweep, f, s + 1, pl.ds(row, 1), lanes]

    small[0].wait()
    for side, row in ((0, 0), (1, chord_cells - 1)):
        for s in range(span_cells):
            cls_edge_out[side, pl.ds(s, 1)] = cls[s + 1, pl.ds(row, 1)]

    for g in range(GROUPS):
        field_loads[g].wait()
        pack_edges(0, g, everything)

    pl.semaphore_wait(barrier, count + len(peers))
    send_class(range(4))
    for g in range(GROUPS):
        send_halo(parcels[0][0], g, range(4))

    for copy in small[1:]:
        copy.wait()
    wall_nodes = pick_node.shape[0]
    values = sens_v[:, 0, :]
    high = values.astype(jnp.bfloat16).astype(jnp.float32)
    split_sens[...] = jnp.concatenate([high, values - high], axis=0).astype(jnp.bfloat16)
    nodes_at = lax.broadcasted_iota(jnp.int32, (wall_nodes, panels), 0)
    pick_node[...] = (nodes_at == node_v[...]).astype(jnp.float32).astype(jnp.bfloat16)

    for turn in range(2):
        core = 1 - my_core if turn == 0 else my_core

        @pl.loop(0, n_x)
        def _(xi):
            rows = []
            for zi in range(n_z):
                mine = (owner_v[...] == xi * (2 * n_z) + zi * 2 + core).astype(jnp.float32).astype(jnp.bfloat16)
                rows.append(split_sens[...] * mine)
            sums = lax.dot_general(
                jnp.concatenate(rows, axis=0), pick_node[...], (((1,), (1,)), ((), ())),
                preferred_element_type=jnp.float32,
            )
            for zi in range(n_z):
                low = 2 * fields * zi
                part[turn, xi, zi] = sums[low : low + fields] + sums[low + fields : low + 2 * fields]

        if turn == 0:
            core_copy().start()
        for g in range(turn * GROUPS // 2, (turn + 1) * GROUPS // 2):
            relay(parcels[0][0], g)

    core_copy().wait_recv()
    part[1] = part[1] + part_core[...]

    for d in range(n_x - 1):
        x_copy(d).start()
    for d in range(4):
        when(exists[opposite[d]], class_copy(d).wait_recv)

    def lookup(index):
        shear_here = jnp.zeros(index.shape, jnp.float32)
        bulk_here = jnp.zeros(index.shape, jnp.float32)
        for level in range(table.shape[1]):
            mask = index == level
            shear_here = jnp.where(mask, table[0, level], shear_here)
            bulk_here = jnp.where(mask, table[1, level], bulk_here)
        return shear_here, bulk_here

    for side in range(2):
        shear_edge[side], bulk_edge[side] = lookup(cls_edge_in[side])

    @pl.loop(0, span_cells + 2)
    def _(s):
        shear[s], bulk[s] = lookup(cls[s])

    row_at = lax.broadcasted_iota(jnp.int32, (chord_cells, depth), 0)
    lane_at = lax.broadcasted_iota(jnp.int32, (chord_cells, depth), 1)

    def beside_chord(values, low, high):
        return (
            jnp.where(row_at == 0, low, pltpu.roll(values, 1, 0)),
            jnp.where(row_at == chord_cells - 1, high, pltpu.roll(values, chord_cells - 1, 0)),
        )

    def beside_depth(values):
        return pltpu.roll(values, 1, 1), pltpu.roll(values, depth - 1, 1)

    @pl.loop(0, span_cells)
    def _(s):
        faces = []
        for coef, edge in ((shear, shear_edge), (bulk, bulk_edge)):
            here = coef[s + 1]
            beside = [coef[s], coef[s + 2]]
            beside += beside_chord(here, edge[0, pl.ds(s, 1)], edge[1, pl.ds(s, 1)])
            low, high = beside_depth(here)
            beside += [jnp.where(lane_at == 0, 0.0, low), jnp.where(lane_at == depth - 1, 0.0, high)]
            faces.append([0.5 * (here + there) for there in beside])
        total = functools.reduce(jnp.add, faces[0])
        for c in range(3):
            weights[12 + c, s] = 1.0 / (total + (faces[1][2 * c] + faces[1][2 * c + 1]))
        for e in range(6):
            normal = faces[0][e] + faces[1][e]
            tangent = faces[0][e]
            if e == 4:
                tangent, normal = (jnp.where(lane_at == 0, 0.0, w) for w in (tangent, normal))
            if e == 5:
                tangent, normal = (jnp.where(lane_at == depth - 1, 0.0, w) for w in (tangent, normal))
            weights[e, s] = tangent
            weights[6 + e, s] = normal

    total = part[1, my_x]
    for d in range(n_x - 1):
        x_copy(d).wait_recv()
        total = total + part_x[d]
    part_z[0] = total
    for d in range(n_z - 1):
        z_copy(d).start()

    steps = chebyshev()

    def slab(sweep, g, s):
        by_diag, by_old = steps[sweep]
        for c in range(3):
            w = [weights[6 + e if e // 2 == c else e, s] for e in range(6)]
            scale = by_diag * weights[12 + c, s]
            for m in range(size // 3):
                f = g * size + (3 * m + c)
                here = u[sweep, f, s + 1]
                row = pl.ds(s, 1)
                beside = [u[sweep, f, s], u[sweep, f, s + 2]]
                beside += beside_chord(here, edge_in[sweep, 0, f, row], edge_in[sweep, 1, f, row])
                beside += beside_depth(here)
                total = src[f, s]
                for e in range(6):
                    total = total + w[e] * beside[e]
                new = scale * total
                if by_old != 0.0:
                    new = new + by_old * u[sweep - 1, f, s + 1]
                if sweep == SWEEPS - 1:
                    out[f, s] = new
                else:
                    u[sweep + 1, f, s + 1] = new
                    edge_out[sweep + 1, 0, f, row] = new[0:1]
                    edge_out[sweep + 1, 1, f, row] = new[chord_cells - 1 : chord_cells]

    source_load.wait()

    @pl.loop(0, GROUPS)
    def _(g):
        receive_halo(0, g, range(4))

        @pl.loop(0, 2)
        def _(i):
            slab(0, g, i * (span_cells - 1))

        send_halo(inner, g, (0, 1))

        @pl.loop(1, span_cells - 1)
        def _(s):
            slab(0, g, s)

        send_halo(inner, g, (2, 3))

        @pl.when(g > 1)
        def _():
            relay(inner, g - 2)

    relay(inner, GROUPS - 2)

    total = part_z[0, my_z]
    for d in range(n_z - 1):
        z_copy(d).wait_recv()
        total = total + part_z[1, d]
    relay(inner, GROUPS - 1)
    wall[...] = jnp.transpose(total)
    at_wall = lax.broadcasted_iota(jnp.int32, (span_cells, chord_cells, 128), 2) == 0
    lanes = pl.ds(0, 128)
    rows = pl.ds(1, span_cells)
    for g in range(GROUPS):
        for c in range(3):
            scale = steps[0][0] * weights[12 + c, :, :, lanes]
            for m in range(size // 3):
                f = g * size + 3 * m + c
                column = wall[:, pl.ds(f, 1)].reshape(span_cells, chord_cells, 1)
                load = jnp.where(at_wall, column, 0.0)
                src[f, :, :, lanes] = src[f, :, :, lanes] + load
                u[1, f, rows, :, lanes] = u[1, f, rows, :, lanes] + scale * load
        send_halo(at_wall_side, g, (0, 1))
        pack_edges(1, g, wall_side)
        send_halo(at_wall_side, g, (2, 3))

    for g in range(GROUPS):
        relay(at_wall_side, g)

    for sweep in range(1, SWEEPS - 1):
        parcel = parcels[sweep + 1][0]

        @pl.loop(0, GROUPS)
        def _(g):
            receive_halo(sweep, g, range(4))

            @pl.loop(0, 2)
            def _(i):
                slab(sweep, g, i * (span_cells - 1))

            send_halo(parcel, g, (0, 1))

            @pl.loop(1, span_cells - 1)
            def _(s):
                slab(sweep, g, s)

            send_halo(parcel, g, (2, 3))

            @pl.when(g > 0)
            def _():
                relay(parcel, g - 1)

    @pl.loop(0, GROUPS)
    def _(g):
        receive_halo(SWEEPS - 1, g, (2, 3))

        @pl.loop(1, span_cells - 1)
        def _(s):
            slab(SWEEPS - 1, g, s)

        @pl.when(g == 0)
        def _():
            relay(parcels[SWEEPS - 1][0], GROUPS - 1)

        receive_halo(SWEEPS - 1, g, (0, 1))

        @pl.loop(0, 2)
        def _(i):
            slab(SWEEPS - 1, g, i * (span_cells - 1))

    for d in range(4):
        when(exists[d], class_copy(d).wait_send)

    for parcel in sum(parcels, []):

        @pl.loop(0, GROUPS)
        def _(g):
            for d in range(4):
                if d < 2:
                    when(
                        far[d],
                        lambda: far_copy(parcel, g, d).wait_send(),
                        lambda: halo_copy(parcel, g, d, True).wait_send(),
                    )
                    when(span == relay_at[d], lambda: hop_copy(parcel, g, d).wait_send())
                    when(exists[d] & jnp.logical_not(far[d]), lambda: halo_copy(parcel, g, d).wait_send())
                else:
                    when(exists[d], lambda: halo_copy(parcel, g, d).wait_send())

    core_copy().wait_send()
    for d in range(n_x - 1):
        x_copy(d).wait_send()
    for d in range(n_z - 1):
        z_copy(d).wait_send()


def body(n_span, n_x, n_z, start, source, classes, table, sens, owner, node):
    fields, span_cells, chord_cells, depth = start.shape
    panels = owner.shape[1]
    wall_nodes = span_cells * chord_cells
    f32, i32, bf16 = jnp.float32, jnp.int32, jnp.bfloat16
    dma = pltpu.SemaphoreType.DMA
    scratch = [
        pltpu.SMEM(table.shape, f32),
        pltpu.VMEM((SWEEPS, fields, span_cells + 2, chord_cells, depth), f32),
        pltpu.VMEM(start.shape, f32),
        pltpu.VMEM((span_cells + 2, chord_cells, depth), i32),
        pltpu.VMEM((fields, 1, panels), f32),
        pltpu.VMEM((1, panels), i32),
        pltpu.VMEM((1, panels), i32),
        pltpu.VMEM((SWEEPS, 2, fields, span_cells, depth), f32),
        pltpu.VMEM((SWEEPS, 2, fields, span_cells, depth), f32),
        pltpu.VMEM((2, span_cells, depth), i32),
        pltpu.VMEM((2, span_cells, depth), i32),
        pltpu.VMEM((SWEEPS, GROUPS, max(RELAYED), chord_cells, depth), f32),
        pltpu.VMEM((span_cells + 2, chord_cells, depth), f32),
        pltpu.VMEM((span_cells + 2, chord_cells, depth), f32),
        pltpu.VMEM((2, span_cells, depth), f32),
        pltpu.VMEM((2, span_cells, depth), f32),
        pltpu.VMEM((15, span_cells, chord_cells, depth), f32),
        pltpu.VMEM((2 * fields, panels), bf16),
        pltpu.VMEM((wall_nodes, panels), bf16),
        pltpu.VMEM((2, n_x, n_z, fields, wall_nodes), f32),
        pltpu.VMEM((n_x, n_z, fields, wall_nodes), f32),
        pltpu.VMEM((n_x - 1, n_z, fields, wall_nodes), f32),
        pltpu.VMEM((2, n_z, fields, wall_nodes), f32),
        pltpu.VMEM((wall_nodes, fields), f32),
        dma((6 + GROUPS,)),
        dma((SWEEPS + 1, GROUPS, 4)),
        dma((SWEEPS + 1, GROUPS, 4)),
        dma((SWEEPS + 1, GROUPS)),
        dma((SWEEPS + 1, GROUPS)),
        dma((SWEEPS + 1, GROUPS)),
        dma((SWEEPS + 1, GROUPS)),
        dma((4,)),
        dma((4,)),
        dma((2,)),
        dma((n_x - 1,)),
        dma((n_x - 1,)),
        dma((n_z - 1,)),
        dma((n_z - 1,)),
    ]
    operands = (start, source, classes, table, sens, owner.reshape(1, panels), node)
    anywhere = pl.BlockSpec(memory_space=pl.ANY)
    return pl.pallas_call(
        functools.partial(kernel, n_span, n_x, n_z),
        out_shape=pltpu.VMEM(start.shape, f32),
        in_specs=[anywhere] * 7,
        out_specs=pl.BlockSpec(memory_space=pltpu.VMEM),
        scratch_shapes=scratch,
        compiler_params=pltpu.CompilerParams(
            collective_id=0, has_side_effects=True, vmem_limit_bytes=48 * 1024 * 1024
        ),
    )(*[pltpu.with_memory_space_constraint(array, pltpu.HBM) for array in operands])


def solution(mesh):
    n_span, n_chord = mesh.shape["span"], mesh.shape["chord"]
    n_x = n_z = round((n_chord // 2) ** 0.5)
    return jax.shard_map(
        functools.partial(body, n_span, n_x, n_z),
        mesh=mesh,
        in_specs=(
            P(None, "span", "chord", None),
            P(None, "span", "chord", None),
            P("span", "chord", None),
            P(),
            P(None, "span", "chord"),
            P("span", "chord", None),
            P("span", "chord"),
        ),
        out_specs=P(None, "span", "chord", None),
        check_vma=False,
    )
```

```python
import functools

import jax
import jax.numpy as jnp
from jax import lax
from jax.experimental import pallas as pl
from jax.experimental.pallas import tpu as pltpu
from jax.sharding import PartitionSpec as P

SWEEPS = 3
GROUPS = 2
RELAYED = (6, 6, 6, 6)
CENTER = 1.0
HALF = 0.9
MESH = pl.DeviceIdType.MESH


def chebyshev():
    rho = HALF / CENTER
    out = [(1.0 / CENTER, 0.0)]
    for _ in range(SWEEPS - 1):
        rho_next = 1.0 / (2.0 * CENTER / HALF - rho)
        out.append((2.0 * rho_next / HALF, -rho_next * rho))
        rho = rho_next
    return out


def kernel(
    n_span, n_x, n_z,
    start, source, classes, table_in, sens, owner, node,
    out,
    table, u, src, cls, sens_v, owner_v, node_v, edge_out, edge_in, cls_edge_out, cls_edge_in, relayed,
    shear, bulk, shear_edge, bulk_edge, weights, split_sens, pick_node, part, part_core, part_x, part_z, wall,
    load_sem, halo_send, halo_recv, far_send, far_recv, hop_send, hop_recv, cls_send, cls_recv, core_sem, x_send, x_recv, z_send, z_recv,
):
    fields, span_cells, chord_cells, depth = start.shape
    panels = owner.shape[1]
    size = fields // GROUPS
    n_chord = 2 * n_x * n_z
    span, chord = lax.axis_index("span"), lax.axis_index("chord")
    my_x, my_z, my_core = chord // (2 * n_z), (chord // 2) % n_z, chord % 2

    def at(xi, zi, core):
        return (span, xi * (2 * n_z) + zi * 2 + core)

    exists = [span > 0, span < n_span - 1, chord > 0, chord < n_chord - 1]
    opposite = [1, 0, 3, 2]
    neighbour = [
        (jnp.maximum(span - 1, 0), chord),
        (jnp.minimum(span + 1, n_span - 1), chord),
        (span, jnp.maximum(chord - 1, 0)),
        (span, jnp.minimum(chord + 1, n_chord - 1)),
    ]
    middle = n_span // 2
    far = [span == middle, span == middle - 1]
    target = [middle - 1, middle]
    middle_of = [middle, middle - 1]
    relay_at = [n_span - 1, 0]
    x_peers = [lax.rem(my_x + d, n_x) for d in range(1, n_x)]
    z_peers = [lax.rem(my_z + d, n_z) for d in range(1, n_z)]

    def group(g, first=0, count=size):
        return pl.ds(g * size + first, count)

    barrier = pltpu.get_barrier_semaphore()
    for d in range(4):

        @pl.when(exists[d])
        def _():
            pl.semaphore_signal(barrier, inc=1, device_id=neighbour[d], device_id_type=MESH)

    for d in range(2):
        for ends in ((middle_of[d], relay_at[d]), (relay_at[d], target[d])):
            for here, there in (ends, ends[::-1]):

                @pl.when(span == here)
                def _():
                    pl.semaphore_signal(barrier, inc=1, device_id=(there, chord), device_id_type=MESH)

    peers = [at(my_x, my_z, 1 - my_core)]
    peers += [at(xi, my_z, my_core) for xi in x_peers] + [at(my_x, zi, my_core) for zi in z_peers]
    for peer in peers:
        pl.semaphore_signal(barrier, inc=1, device_id=peer, device_id_type=MESH)
    count = sum(jnp.where(exists[d], 1, 0) for d in range(4))
    count = count + sum(jnp.where(far[d], 2, 0) + jnp.where(span == relay_at[d], 2, 0) for d in range(2))

    small = [
        pltpu.make_async_copy(classes, cls.at[pl.ds(1, span_cells)], load_sem.at[0]),
        pltpu.make_async_copy(table_in, table, load_sem.at[5 + GROUPS]),
        pltpu.make_async_copy(owner, owner_v, load_sem.at[1]),
        pltpu.make_async_copy(node, node_v, load_sem.at[2]),
        pltpu.make_async_copy(sens, sens_v, load_sem.at[3]),
    ]
    field_loads = [
        pltpu.make_async_copy(
            start.at[pl.ds(g * size, size)],
            u.at[0, pl.ds(g * size, size), pl.ds(1, span_cells)],
            load_sem.at[4 + g],
        )
        for g in range(GROUPS)
    ]
    source_load = pltpu.make_async_copy(source, src, load_sem.at[4 + GROUPS])
    for copy in small + field_loads + [source_load]:
        copy.start()

    @pl.when(jnp.logical_not(exists[0]))
    def _():
        cls[0] = jnp.full(cls.shape[1:], -1, jnp.int32)
        for s in range(SWEEPS):
            for f in range(fields):
                u[s, f, 0] = jnp.zeros((chord_cells, depth), jnp.float32)

    @pl.when(jnp.logical_not(exists[1]))
    def _():
        cls[span_cells + 1] = jnp.full(cls.shape[1:], -1, jnp.int32)
        for s in range(SWEEPS):
            for f in range(fields):
                u[s, f, span_cells + 1] = jnp.zeros((chord_cells, depth), jnp.float32)

    for side in range(2):

        @pl.when(jnp.logical_not(exists[2 + side]))
        def _():
            cls_edge_in[side] = jnp.full(cls_edge_in.shape[1:], -1, jnp.int32)
            for s in range(SWEEPS):
                edge_in[s, side] = jnp.zeros(edge_in.shape[2:], jnp.float32)

    def class_copy(d):
        if d < 2:
            row = 0 if d == 0 else span_cells - 1
            from_ref = classes.at[pl.ds(row, 1)]
            to_ref = cls.at[pl.ds(span_cells + 1 if d == 0 else 0, 1)]
        else:
            from_ref, to_ref = cls_edge_out.at[d - 2], cls_edge_in.at[opposite[d] - 2]
        return pltpu.make_async_remote_copy(
            src_ref=from_ref, dst_ref=to_ref, send_sem=cls_send.at[d], recv_sem=cls_recv.at[d],
            device_id=neighbour[d], device_id_type=MESH,
        )

    everything, wall_side, inner_side = pl.ds(0, depth), pl.ds(0, depth // 2), pl.ds(depth // 2, depth // 2)
    inner, at_wall_side = (1, inner_side, SWEEPS), (1, wall_side, 1)
    parcels = [[(s, everything, s)] if s != 1 else [inner, at_wall_side] for s in range(SWEEPS)]

    def outer_row(parcel, d, some):
        sweep, lanes, _ = parcel
        row = 0 if d == 0 else span_cells - 1
        return start.at[some, row, :, lanes] if sweep == 0 else u.at[sweep, some, row + 1, :, lanes]

    def halo_row(parcel, d, some):
        sweep, lanes, _ = parcel
        return u.at[sweep, some, span_cells + 1 if d == 0 else 0, :, lanes]

    def halo_copy(parcel, g, d, relay_too=False):
        sweep, lanes, slot = parcel
        if d < 2:
            some = group(g, 0, size - RELAYED[slot] if relay_too else size)
            from_ref, to_ref = outer_row(parcel, d, some), halo_row(parcel, d, some)
        else:
            from_ref = edge_out.at[sweep, d - 2, group(g), :, lanes]
            to_ref = edge_in.at[sweep, opposite[d] - 2, group(g), :, lanes]
        return pltpu.make_async_remote_copy(
            src_ref=from_ref, dst_ref=to_ref, send_sem=halo_send.at[slot, g, d], recv_sem=halo_recv.at[slot, g, d],
            device_id=neighbour[d], device_id_type=MESH,
        )

    def relay_fields(slot, g):
        return group(g, size - RELAYED[slot], RELAYED[slot])

    def far_copy(parcel, g, d):
        sweep, lanes, slot = parcel
        return pltpu.make_async_remote_copy(
            src_ref=outer_row(parcel, d, relay_fields(slot, g)),
            dst_ref=relayed.at[sweep, g, pl.ds(0, RELAYED[slot]), :, lanes],
            send_sem=far_send.at[slot, g], recv_sem=far_recv.at[slot, g],
            device_id=(relay_at[d], chord), device_id_type=MESH,
        )

    def hop_copy(parcel, g, d):
        sweep, lanes, slot = parcel
        return pltpu.make_async_remote_copy(
            src_ref=relayed.at[sweep, g, pl.ds(0, RELAYED[slot]), :, lanes],
            dst_ref=halo_row(parcel, d, relay_fields(slot, g)),
            send_sem=hop_send.at[slot, g], recv_sem=hop_recv.at[slot, g],
            device_id=(target[d], chord), device_id_type=MESH,
        )

    def when(condition, *actions):
        @pl.when(condition)
        def _():
            for action in actions:
                action()

    def send_class(directions):
        for d in directions:
            when(exists[d], class_copy(d).start)

    def send_halo(parcel, g, directions):
        for d in directions:
            if d < 2:
                when(far[d], lambda: far_copy(parcel, g, d).start(), lambda: halo_copy(parcel, g, d, True).start())
                when(exists[d] & jnp.logical_not(far[d]), lambda: halo_copy(parcel, g, d).start())
            else:
                when(exists[d], lambda: halo_copy(parcel, g, d).start())

    def receive_halo(sweep, g, directions):
        for d in directions:
            back = opposite[d]
            for parcel in parcels[sweep]:
                if d < 2:
                    when(
                        far[back],
                        lambda: halo_copy(parcel, g, d, True).wait_recv(),
                        lambda: hop_copy(parcel, g, d).wait_recv(),
                    )
                    when(exists[back] & jnp.logical_not(far[back]), lambda: halo_copy(parcel, g, d).wait_recv())
                else:
                    when(exists[back], lambda: halo_copy(parcel, g, d).wait_recv())

    def relay(parcel, g):
        for d in range(2):
            when(span == relay_at[d], lambda: far_copy(parcel, g, d).wait_recv(), lambda: hop_copy(parcel, g, d).start())

    def core_copy():
        return pltpu.make_async_remote_copy(
            src_ref=part.at[0], dst_ref=part_core, send_sem=core_sem.at[0], recv_sem=core_sem.at[1],
            device_id=at(my_x, my_z, 1 - my_core), device_id_type=MESH,
        )

    def x_copy(d):
        return pltpu.make_async_remote_copy(
            src_ref=part.at[1, x_peers[d]], dst_ref=part_x.at[d], send_sem=x_send.at[d], recv_sem=x_recv.at[d],
            device_id=at(x_peers[d], my_z, my_core), device_id_type=MESH,
        )

    def z_copy(d):
        return pltpu.make_async_remote_copy(
            src_ref=part_z.at[0, z_peers[d]], dst_ref=part_z.at[1, d], send_sem=z_send.at[d], recv_sem=z_recv.at[d],
            device_id=at(my_x, z_peers[d], my_core), device_id_type=MESH,
        )

    def pack_edges(sweep, g, lanes):
        @pl.loop(g * size, (g + 1) * size)
        def _(f):
            for side, row in ((0, 0), (1, chord_cells - 1)):
                for s in range(span_cells):
                    edge_out[sweep, side, f, pl.ds(s, 1), lanes] = u[sweep, f, s + 1, pl.ds(row, 1), lanes]

    small[0].wait()
    for side, row in ((0, 0), (1, chord_cells - 1)):
        for s in range(span_cells):
            cls_edge_out[side, pl.ds(s, 1)] = cls[s + 1, pl.ds(row, 1)]

    for g in range(GROUPS):
        field_loads[g].wait()
        pack_edges(0, g, everything)

    pl.semaphore_wait(barrier, count + len(peers))
    send_class(range(4))
    for g in range(GROUPS):
        send_halo(parcels[0][0], g, range(4))

    for copy in small[1:]:
        copy.wait()
    wall_nodes = pick_node.shape[0]
    values = sens_v[:, 0, :]
    high = values.astype(jnp.bfloat16).astype(jnp.float32)
    split_sens[...] = jnp.concatenate([high, values - high], axis=0).astype(jnp.bfloat16)
    nodes_at = lax.broadcasted_iota(jnp.int32, (wall_nodes, panels), 0)
    pick_node[...] = (nodes_at == node_v[...]).astype(jnp.float32).astype(jnp.bfloat16)

    for turn in range(2):
        core = 1 - my_core if turn == 0 else my_core

        @pl.loop(0, n_x)
        def _(xi):
            rows = []
            for zi in range(n_z):
                mine = (owner_v[...] == xi * (2 * n_z) + zi * 2 + core).astype(jnp.float32).astype(jnp.bfloat16)
                rows.append(split_sens[...] * mine)
            sums = lax.dot_general(
                jnp.concatenate(rows, axis=0), pick_node[...], (((1,), (1,)), ((), ())),
                preferred_element_type=jnp.float32,
            )
            for zi in range(n_z):
                low = 2 * fields * zi
                part[turn, xi, zi] = sums[low : low + fields] + sums[low + fields : low + 2 * fields]

        if turn == 0:
            core_copy().start()
        for g in range(turn * GROUPS // 2, (turn + 1) * GROUPS // 2):
            relay(parcels[0][0], g)

    core_copy().wait_recv()
    part[1] = part[1] + part_core[...]

    for d in range(n_x - 1):
        x_copy(d).start()
    for d in range(4):
        when(exists[opposite[d]], class_copy(d).wait_recv)

    def lookup(index):
        shear_here = jnp.zeros(index.shape, jnp.float32)
        bulk_here = jnp.zeros(index.shape, jnp.float32)
        for level in range(table.shape[1]):
            mask = index == level
            shear_here = jnp.where(mask, table[0, level], shear_here)
            bulk_here = jnp.where(mask, table[1, level], bulk_here)
        return shear_here, bulk_here

    for side in range(2):
        shear_edge[side], bulk_edge[side] = lookup(cls_edge_in[side])

    @pl.loop(0, span_cells + 2)
    def _(s):
        shear[s], bulk[s] = lookup(cls[s])

    row_at = lax.broadcasted_iota(jnp.int32, (chord_cells, depth), 0)
    lane_at = lax.broadcasted_iota(jnp.int32, (chord_cells, depth), 1)

    def beside_chord(values, low, high):
        return (
            jnp.where(row_at == 0, low, pltpu.roll(values, 1, 0)),
            jnp.where(row_at == chord_cells - 1, high, pltpu.roll(values, chord_cells - 1, 0)),
        )

    def beside_depth(values):
        return pltpu.roll(values, 1, 1), pltpu.roll(values, depth - 1, 1)

    @pl.loop(0, span_cells)
    def _(s):
        faces = []
        for coef, edge in ((shear, shear_edge), (bulk, bulk_edge)):
            here = coef[s + 1]
            beside = [coef[s], coef[s + 2]]
            beside += beside_chord(here, edge[0, pl.ds(s, 1)], edge[1, pl.ds(s, 1)])
            low, high = beside_depth(here)
            beside += [jnp.where(lane_at == 0, 0.0, low), jnp.where(lane_at == depth - 1, 0.0, high)]
            faces.append([0.5 * (here + there) for there in beside])
        total = functools.reduce(jnp.add, faces[0])
        for c in range(3):
            weights[12 + c, s] = 1.0 / (total + (faces[1][2 * c] + faces[1][2 * c + 1]))
        for e in range(6):
            normal = faces[0][e] + faces[1][e]
            tangent = faces[0][e]
            if e == 4:
                tangent, normal = (jnp.where(lane_at == 0, 0.0, w) for w in (tangent, normal))
            if e == 5:
                tangent, normal = (jnp.where(lane_at == depth - 1, 0.0, w) for w in (tangent, normal))
            weights[e, s] = tangent
            weights[6 + e, s] = normal

    total = part[1, my_x]
    for d in range(n_x - 1):
        x_copy(d).wait_recv()
        total = total + part_x[d]
    part_z[0] = total
    for d in range(n_z - 1):
        z_copy(d).start()

    steps = chebyshev()

    def slab(sweep, g, s):
        by_diag, by_old = steps[sweep]
        for c in range(3):
            w = [weights[6 + e if e // 2 == c else e, s] for e in range(6)]
            scale = by_diag * weights[12 + c, s]
            for m in range(size // 3):
                f = g * size + (3 * m + c)
                here = u[sweep, f, s + 1]
                row = pl.ds(s, 1)
                beside = [u[sweep, f, s], u[sweep, f, s + 2]]
                beside += beside_chord(here, edge_in[sweep, 0, f, row], edge_in[sweep, 1, f, row])
                beside += beside_depth(here)
                total = src[f, s]
                for e in range(6):
                    total = total + w[e] * beside[e]
                new = scale * total
                if by_old != 0.0:
                    new = new + by_old * u[sweep - 1, f, s + 1]
                if sweep == SWEEPS - 1:
                    out[f, s] = new
                else:
                    u[sweep + 1, f, s + 1] = new
                    edge_out[sweep + 1, 0, f, row] = new[0:1]
                    edge_out[sweep + 1, 1, f, row] = new[chord_cells - 1 : chord_cells]

    source_load.wait()

    @pl.loop(0, GROUPS)
    def _(g):
        receive_halo(0, g, range(4))

        @pl.loop(0, 2)
        def _(i):
            slab(0, g, i * (span_cells - 1))

        send_halo(inner, g, (0, 1))

        @pl.loop(1, span_cells - 1)
        def _(s):
            slab(0, g, s)

        send_halo(inner, g, (2, 3))

        @pl.when(g > 1)
        def _():
            relay(inner, g - 2)

    relay(inner, GROUPS - 2)

    total = part_z[0, my_z]
    for d in range(n_z - 1):
        z_copy(d).wait_recv()
        total = total + part_z[1, d]
    relay(inner, GROUPS - 1)
    wall[...] = jnp.transpose(total)
    at_wall = lax.broadcasted_iota(jnp.int32, (span_cells, chord_cells, 128), 2) == 0
    lanes = pl.ds(0, 128)
    rows = pl.ds(1, span_cells)
    for g in range(GROUPS):
        for c in range(3):
            scale = steps[0][0] * weights[12 + c, :, :, lanes]
            for m in range(size // 3):
                f = g * size + 3 * m + c
                column = wall[:, pl.ds(f, 1)].reshape(span_cells, chord_cells, 1)
                load = jnp.where(at_wall, column, 0.0)
                src[f, :, :, lanes] = src[f, :, :, lanes] + load
                u[1, f, rows, :, lanes] = u[1, f, rows, :, lanes] + scale * load
        send_halo(at_wall_side, g, (0, 1))
        pack_edges(1, g, wall_side)
        send_halo(at_wall_side, g, (2, 3))

    for g in range(GROUPS):
        relay(at_wall_side, g)

    for sweep in range(1, SWEEPS - 1):
        parcel = parcels[sweep + 1][0]

        @pl.loop(0, GROUPS)
        def _(g):
            @pl.when(g > 0)
            def _():
                relay(parcel, g - 1)

            receive_halo(sweep, g, range(4))

            @pl.loop(0, 2)
            def _(i):
                slab(sweep, g, i * (span_cells - 1))

            send_halo(parcel, g, (0, 1))

            @pl.loop(1, span_cells - 1)
            def _(s):
                slab(sweep, g, s)

            send_halo(parcel, g, (2, 3))

    @pl.loop(0, GROUPS)
    def _(g):
        receive_halo(SWEEPS - 1, g, (2, 3))

        @pl.loop(1, span_cells - 1)
        def _(s):
            slab(SWEEPS - 1, g, s)

        @pl.when(g == 0)
        def _():
            relay(parcels[SWEEPS - 1][0], GROUPS - 1)

        receive_halo(SWEEPS - 1, g, (0, 1))

        @pl.loop(0, 2)
        def _(i):
            slab(SWEEPS - 1, g, i * (span_cells - 1))

    for d in range(4):
        when(exists[d], class_copy(d).wait_send)

    for parcel in sum(parcels, []):

        @pl.loop(0, GROUPS)
        def _(g):
            for d in range(4):
                if d < 2:
                    when(
                        far[d],
                        lambda: far_copy(parcel, g, d).wait_send(),
                        lambda: halo_copy(parcel, g, d, True).wait_send(),
                    )
                    when(span == relay_at[d], lambda: hop_copy(parcel, g, d).wait_send())
                    when(exists[d] & jnp.logical_not(far[d]), lambda: halo_copy(parcel, g, d).wait_send())
                else:
                    when(exists[d], lambda: halo_copy(parcel, g, d).wait_send())

    core_copy().wait_send()
    for d in range(n_x - 1):
        x_copy(d).wait_send()
    for d in range(n_z - 1):
        z_copy(d).wait_send()


def body(n_span, n_x, n_z, start, source, classes, table, sens, owner, node):
    fields, span_cells, chord_cells, depth = start.shape
    panels = owner.shape[1]
    wall_nodes = span_cells * chord_cells
    f32, i32, bf16 = jnp.float32, jnp.int32, jnp.bfloat16
    dma = pltpu.SemaphoreType.DMA
    scratch = [
        pltpu.SMEM(table.shape, f32),
        pltpu.VMEM((SWEEPS, fields, span_cells + 2, chord_cells, depth), f32),
        pltpu.VMEM(start.shape, f32),
        pltpu.VMEM((span_cells + 2, chord_cells, depth), i32),
        pltpu.VMEM((fields, 1, panels), f32),
        pltpu.VMEM((1, panels), i32),
        pltpu.VMEM((1, panels), i32),
        pltpu.VMEM((SWEEPS, 2, fields, span_cells, depth), f32),
        pltpu.VMEM((SWEEPS, 2, fields, span_cells, depth), f32),
        pltpu.VMEM((2, span_cells, depth), i32),
        pltpu.VMEM((2, span_cells, depth), i32),
        pltpu.VMEM((SWEEPS, GROUPS, max(RELAYED), chord_cells, depth), f32),
        pltpu.VMEM((span_cells + 2, chord_cells, depth), f32),
        pltpu.VMEM((span_cells + 2, chord_cells, depth), f32),
        pltpu.VMEM((2, span_cells, depth), f32),
        pltpu.VMEM((2, span_cells, depth), f32),
        pltpu.VMEM((15, span_cells, chord_cells, depth), f32),
        pltpu.VMEM((2 * fields, panels), bf16),
        pltpu.VMEM((wall_nodes, panels), bf16),
        pltpu.VMEM((2, n_x, n_z, fields, wall_nodes), f32),
        pltpu.VMEM((n_x, n_z, fields, wall_nodes), f32),
        pltpu.VMEM((n_x - 1, n_z, fields, wall_nodes), f32),
        pltpu.VMEM((2, n_z, fields, wall_nodes), f32),
        pltpu.VMEM((wall_nodes, fields), f32),
        dma((6 + GROUPS,)),
        dma((SWEEPS + 1, GROUPS, 4)),
        dma((SWEEPS + 1, GROUPS, 4)),
        dma((SWEEPS + 1, GROUPS)),
        dma((SWEEPS + 1, GROUPS)),
        dma((SWEEPS + 1, GROUPS)),
        dma((SWEEPS + 1, GROUPS)),
        dma((4,)),
        dma((4,)),
        dma((2,)),
        dma((n_x - 1,)),
        dma((n_x - 1,)),
        dma((n_z - 1,)),
        dma((n_z - 1,)),
    ]
    operands = (start, source, classes, table, sens, owner.reshape(1, panels), node)
    anywhere = pl.BlockSpec(memory_space=pl.ANY)
    return pl.pallas_call(
        functools.partial(kernel, n_span, n_x, n_z),
        out_shape=pltpu.VMEM(start.shape, f32),
        in_specs=[anywhere] * 7,
        out_specs=pl.BlockSpec(memory_space=pltpu.VMEM),
        scratch_shapes=scratch,
        compiler_params=pltpu.CompilerParams(
            collective_id=0, has_side_effects=True, vmem_limit_bytes=48 * 1024 * 1024
        ),
    )(*[pltpu.with_memory_space_constraint(array, pltpu.HBM) for array in operands])


def solution(mesh):
    n_span, n_chord = mesh.shape["span"], mesh.shape["chord"]
    n_x = n_z = round((n_chord // 2) ** 0.5)
    return jax.shard_map(
        functools.partial(body, n_span, n_x, n_z),
        mesh=mesh,
        in_specs=(
            P(None, "span", "chord", None),
            P(None, "span", "chord", None),
            P("span", "chord", None),
            P(),
            P(None, "span", "chord"),
            P("span", "chord", None),
            P("span", "chord"),
        ),
        out_specs=P(None, "span", "chord", None),
        check_vma=False,
    )
```
